32 devices in a mesh: fsdp: 16 (over z, y, core), mp: 2 (over x).
Axes of the slice: x: 2, y: 2, z: 4, core: 2. Of those that a mesh axis runs over, the one named last changes fastest.
Arguments:
- tokens: bfloat16 [8192, 3072], P('fsdp', 'mp'), may hold values from -6 to 6
- ln_gain: float32 [3072], replicated, may hold values from 0.1 to 1.9
- w_qkv: bfloat16 [3072, 3, 3072], P('fsdp', None, 'mp'), may hold values from -0.109375 to 0.109375
- w_up: bfloat16 [3072, 12288], P('fsdp', 'mp'), may hold values from -0.109375 to 0.109375
- q_gain: float32 [24, 128], P('mp'), may hold values from 0.4 to 16
- k_gain: float32 [24, 128], P('mp'), may hold values from 0.4 to 16
- w_proj: bfloat16 [3072, 3072], P('mp', 'fsdp'), may hold values from -0.109375 to 0.109375
- w_down: bfloat16 [12288, 3072], P('mp', 'fsdp'), may hold values from -0.0546875 to 0.0546875
Outputs:
- block_out: bfloat16 [8192, 3072], P('fsdp', 'mp')
The draws below stay inside these ranges and needn't reach their ends.
All inputs are finite; a program needn't handle non-finite values.
Results may differ from the reference program's by a relative error of at most 0.015.
Values may be sent and summed in bfloat16 or wider, within the bound.
A program may use at most 192 MiB of HBM per device.

```python
import jax
import jax.numpy as jnp
from jax import lax

H = 24
HD = 128
FF = 12288
PATCHES = 256
D = 3072
TOKENS = 8192
N_MP = 2


def draw_gain_table(key, low_head, high_head):
    head_key, entry_key = jax.random.split(key)
    head_scale = jnp.exp(jax.random.uniform(head_key, (H, 1), jnp.float32, jnp.log(low_head), jnp.log(high_head)))
    entries = jax.random.uniform(entry_key, (H, HD), jnp.float32, 0.6, 1.5)
    return entries * head_scale


def draw_q_gain(key, part):
    key = jax.random.fold_in(key, 11)
    return draw_gain_table(key, 0.8, 1.6)


def draw_k_gain(key, part):
    key = jax.random.fold_in(key, 23)
    return draw_gain_table(key, 0.8, 1.6)


def block_scale(rng, extent, pieces, smallest, high):
    loudness = 1.0
    for axis_at, blocks in pieces:
        heights = jax.random.uniform(jax.random.fold_in(jax.random.fold_in(rng, 6), axis_at), (blocks,), jnp.float32, smallest / len(pieces), high / len(pieces))
        loudness = loudness * jnp.repeat(jnp.exp(heights), extent[axis_at] // blocks).reshape((-1,) + (1,) * (len(extent) - 1 - axis_at))
    return loudness


def normal_values(own_key, extent, deviation, bound, cuts=(), kind=jnp.bfloat16):
    level = block_scale(own_key, extent, cuts, -0.22, 0.18) if cuts else 1.0
    values = jax.random.normal(own_key, extent, jnp.float32) * deviation * level
    return jnp.minimum(jnp.maximum(values, -bound), bound).astype(kind)


def setup_inputs(seed: int = 0) -> dict:
    key_of = jax.random.split(jax.random.key(seed), 9)
    return {
        "tokens": normal_values(key_of[0], (TOKENS, D), 1.0, 6.0, ((0, 16), (1, 2))),
        "ln_gain": jnp.clip(1.0 + 0.18 * jax.random.normal(key_of[1], (D,), jnp.float32), 0.1, 1.9),
        "w_qkv": normal_values(key_of[2], (D, 3, H * HD), D ** -0.5, 0.109375, ((0, 16), (2, 2))),
        "w_up": normal_values(key_of[3], (D, FF), D ** -0.5, 0.109375, ((0, 16), (1, 2))),
        "q_gain": draw_q_gain(jax.random.fold_in(key_of[8], 71), 0),
        "k_gain": draw_k_gain(jax.random.fold_in(key_of[8], 71), 0),
        "w_proj": normal_values(key_of[6], (H * HD, D), (H * HD) ** -0.5, 0.109375, ((0, 2), (1, 16))),
        "w_down": normal_values(key_of[7], (FF, D), FF ** -0.5, 0.0546875, ((0, 2), (1, 16))),
    }


def layer_norm(values, gain):
    mean = lax.optimization_barrier(jnp.mean(values, axis=-1, keepdims=True))
    centred = values - mean
    variance = lax.optimization_barrier(jnp.mean(centred * centred, axis=-1, keepdims=True))
    return centred * lax.rsqrt(variance + 1e-06) * gain

def one_image(inputs):
    queries, keys, values = inputs
    scores = jnp.einsum('qhd,khd->hqk', queries.astype(jnp.float32), keys.astype(jnp.float32)) * HD ** (-0.5)
    scores = scores - lax.optimization_barrier(jnp.max(scores, axis=-1, keepdims=True))
    weights = jnp.exp(scores)
    probs = (weights / lax.optimization_barrier(jnp.sum(weights, axis=-1, keepdims=True))).astype(jnp.bfloat16)
    mixed = jnp.einsum('hqk,khd->qhd', probs.astype(jnp.float32), values.astype(jnp.float32))
    return mixed.astype(jnp.bfloat16)

def reference(tokens, ln_gain, w_qkv, w_up, q_gain, k_gain, w_proj, w_down):
    rows = tokens.astype(jnp.float32)
    normed = layer_norm(rows, ln_gain).astype(jnp.bfloat16)
    projected = jnp.einsum('td,dca->cta', normed.astype(jnp.float32), w_qkv.astype(jnp.float32))
    images = TOKENS // PATCHES
    queries = layer_norm(projected[0].reshape(TOKENS, H, HD), q_gain).astype(jnp.bfloat16)
    keys = layer_norm(projected[1].reshape(TOKENS, H, HD), k_gain).astype(jnp.bfloat16)
    values = projected[2].reshape(TOKENS, H, HD).astype(jnp.bfloat16)
    attended = lax.map(one_image, (queries.reshape(images, PATCHES, H, HD), keys.reshape(images, PATCHES, H, HD), values.reshape(images, PATCHES, H, HD)))
    attended = attended.reshape(TOKENS, H * HD)
    hidden_pre = jnp.dot(normed, w_up, preferred_element_type=jnp.float32)
    activated = jax.nn.gelu(hidden_pre, approximate=False).astype(jnp.bfloat16)
    width_attn = H * HD // N_MP
    width_mlp = FF // N_MP
    branches = jnp.zeros((TOKENS, D), jnp.float32)
    for group in range(N_MP):
        term = jnp.dot(attended[:, group * width_attn:(group + 1) * width_attn], w_proj[group * width_attn:(group + 1) * width_attn], preferred_element_type=jnp.float32)
        term = term + jnp.dot(activated[:, group * width_mlp:(group + 1) * width_mlp], w_down[group * width_mlp:(group + 1) * width_mlp], preferred_element_type=jnp.float32)
        rounded = lax.optimization_barrier(term.astype(jnp.bfloat16))
        branches = branches + rounded.astype(jnp.float32)
    return (rows + branches).astype(jnp.bfloat16)
```

```python
import jax
import jax.numpy as jnp
from jax import lax
from jax.sharding import PartitionSpec as P

HD = 128
PATCHES = 256


def layer_norm(values, gain):
    mean = jnp.mean(values, axis=-1, keepdims=True)
    centred = values - mean
    variance = jnp.mean(centred * centred, axis=-1, keepdims=True)
    return centred * lax.rsqrt(variance + 1e-06) * gain


def attention(projected, q_gain, k_gain):
    tok_count = projected[0].shape[0]
    heads = q_gain.shape[0]
    images = tok_count // PATCHES
    queries = layer_norm(projected[0].reshape(tok_count, heads, HD), q_gain)
    keys = layer_norm(projected[1].reshape(tok_count, heads, HD), k_gain)
    split = (images, PATCHES, heads, HD)
    queries = queries.astype(jnp.bfloat16).reshape(split)
    keys = keys.astype(jnp.bfloat16).reshape(split)
    values = projected[2].astype(jnp.bfloat16).reshape(split)
    scores = jnp.einsum(
        "iqhd,ikhd->ihqk", queries, keys, preferred_element_type=jnp.float32
    ) * HD ** (-0.5)
    scores = scores - jnp.max(scores, axis=-1, keepdims=True)
    weights = jnp.exp(scores)
    probs = (weights / jnp.sum(weights, axis=-1, keepdims=True)).astype(jnp.bfloat16)
    attended = jnp.einsum("ihqk,ikhd->iqhd", probs, values, preferred_element_type=jnp.float32)
    return attended.astype(jnp.bfloat16).reshape(tok_count, heads * HD)


def gathered(tokens, ln_gain, w_qkv, w_up, q_gain, k_gain, w_proj, w_down):
    rows = tokens.astype(jnp.float32)
    panels = lax.all_gather(tokens, "mp", axis=1, tiled=True)
    normed = layer_norm(panels.astype(jnp.float32), ln_gain).astype(jnp.bfloat16)
    projected = jnp.einsum(
        "td,dca->cta",
        normed,
        lax.all_gather(w_qkv, "fsdp", axis=0, tiled=True),
        preferred_element_type=jnp.float32,
    )
    hidden_pre = jnp.dot(
        normed,
        lax.all_gather(w_up, "fsdp", axis=0, tiled=True),
        preferred_element_type=jnp.float32,
    )
    attended = attention(projected, q_gain, k_gain)
    activated = jax.nn.gelu(hidden_pre, approximate=False).astype(jnp.bfloat16)
    joined = jnp.concatenate([attended, activated], axis=1)
    out_rows = jnp.concatenate([w_proj, w_down], axis=0)
    terms = jnp.dot(
        joined,
        lax.all_gather(out_rows, "fsdp", axis=1, tiled=True),
        preferred_element_type=jnp.float32,
    )
    branches = lax.psum_scatter(
        terms.astype(jnp.bfloat16), "mp", scatter_dimension=1, tiled=True
    ).astype(jnp.float32)
    return (rows + branches).astype(jnp.bfloat16)


def paired(n):
    planes = n // 4
    core_bit, y_bit, z_bit = 1, 2, 4

    def swap(value, mask, axis="fsdp"):
        count = n if axis == "fsdp" else 2
        return lax.ppermute(value, axis, [(i, i ^ mask) for i in range(count)])

    def local(tokens, ln_gain, w_qkv, w_up, q_gain, k_gain, w_proj, w_down):
        me = lax.axis_index("fsdp")
        side = lax.axis_index("mp")
        half = (me // z_bit) % 2
        tok_count = tokens.shape[0]
        depth = w_up.shape[0]
        heads = q_gain.shape[0] // 2
        head_cols, hidden = heads * HD, w_up.shape[1] // 2

        def in_half(which):
            qkv = lax.dynamic_slice_in_dim(w_qkv, which * head_cols, head_cols, 2)
            up = lax.dynamic_slice_in_dim(w_up, which * hidden, hidden, 1)
            return jnp.concatenate([qkv.reshape(depth, 3 * head_cols), up], axis=1)

        def out_half(which):
            proj = lax.dynamic_slice_in_dim(w_proj, which * head_cols, head_cols, 0)
            down = lax.dynamic_slice_in_dim(w_down, which * hidden, hidden, 0)
            return jnp.concatenate([proj, down], axis=0).T

        def spread(make_half, after):
            mine, other = make_half(half), make_half(1 - half)
            if after:
                mine, other, _ = lax.optimization_barrier((mine, other, after))
            blocks = []
            for k in range(planes):
                here = mine if k == 0 else swap(other if k % 2 else mine, k * z_bit)
                across = swap(here, y_bit)
                blocks.append([here, swap(here, core_bit), across, swap(across, core_bit)])
            return blocks

        both = jnp.concatenate([tokens, swap(tokens, z_bit)], axis=0)
        peer = swap(both, 1, "mp")
        first = jnp.where(side == 0, both, peer)
        second = jnp.where(side == 0, peer, both)
        panels = jnp.concatenate([first, second], axis=1)
        normed = layer_norm(panels.astype(jnp.float32), ln_gain).astype(jnp.bfloat16)

        in_blocks = spread(in_half, ())
        out_blocks = spread(out_half, [blocks[0] for blocks in in_blocks[1:]])

        w_in = jnp.zeros((n, depth, 3 * head_cols + hidden), jnp.bfloat16)
        for k in range(planes):
            for j in range(4):
                w_in = lax.dynamic_update_slice_in_dim(
                    w_in, in_blocks[k][j][None], me ^ (k * z_bit + j), 0
                )
        w_in = w_in.reshape(n * depth, 3 * head_cols + hidden)
        projected = [
            jnp.dot(
                normed,
                w_in[:, c * head_cols : (c + 1) * head_cols],
                preferred_element_type=jnp.float32,
            )
            for c in range(3)
        ]
        gain_q = lax.dynamic_slice_in_dim(q_gain, half * heads, heads, 0)
        gain_k = lax.dynamic_slice_in_dim(k_gain, half * heads, heads, 0)
        attended = attention(projected, gain_q, gain_k)
        hidden_pre = jnp.dot(
            normed, w_in[:, 3 * head_cols :], preferred_element_type=jnp.float32
        )
        activated = jax.nn.gelu(hidden_pre, approximate=False).astype(jnp.bfloat16)
        joined = jnp.concatenate([attended, activated], axis=1)

        def term(k):
            w_out = jnp.zeros((4, depth, joined.shape[1]), jnp.bfloat16)
            for j in range(4):
                w_out = lax.dynamic_update_slice_in_dim(
                    w_out, out_blocks[k][j][None], (me % 4) ^ j, 0
                )
            return lax.dot_general(
                joined,
                w_out.reshape(4 * depth, joined.shape[1]),
                (((1,), (1,)), ((), ())),
                preferred_element_type=jnp.float32,
            ).astype(jnp.bfloat16)

        keep_low = (me // (2 * z_bit)) % 2 == side
        own, far = [], []
        for stage in range(2):
            low, high = term(stage), term(stage + 2)
            keep = jnp.where(keep_low, low, high)
            got = swap(jnp.where(keep_low, high, low), 1, "mp")
            total = keep.astype(jnp.float32) + got.astype(jnp.float32)
            own.append(total[:tok_count])
            far.append(swap(total[tok_count:].astype(jnp.bfloat16), z_bit))
        done = [own[s] + far[1 - s].astype(jnp.float32) for s in range(2)]
        branches = jnp.where(
            half == 0,
            jnp.concatenate(done, axis=1),
            jnp.concatenate(done[::-1], axis=1),
        )
        return (tokens.astype(jnp.float32) + branches).astype(jnp.bfloat16)

    return local


def solution(mesh):
    n, sides = mesh.shape["fsdp"], mesh.shape["mp"]
    return jax.shard_map(
        paired(n) if (n, sides) == (16, 2) else gathered,
        mesh=mesh,
        in_specs=(
            P("fsdp", "mp"),
            P(),
            P("fsdp", None, "mp"),
            P("fsdp", "mp"),
            P("mp", None),
            P("mp", None),
            P("mp", "fsdp"),
            P("mp", "fsdp"),
        ),
        out_specs=P("fsdp", "mp"),
        check_vma=False,
    )
```

```python
import jax
import jax.numpy as jnp
from jax import lax
from jax.experimental import pallas as pl
from jax.experimental.pallas import tpu as pltpu
from jax.sharding import PartitionSpec as P

HD = 128
PATCHES = 256


def layer_norm(values, gain):
    mean = jnp.mean(values, axis=-1, keepdims=True)
    centred = values - mean
    variance = jnp.mean(centred * centred, axis=-1, keepdims=True)
    return centred * lax.rsqrt(variance + 1e-06) * gain


def attention(projected, q_gain, k_gain):
    tok_count = projected[0].shape[0]
    heads = q_gain.shape[0]
    images = tok_count // PATCHES
    queries = layer_norm(projected[0].reshape(tok_count, heads, HD), q_gain)
    keys = layer_norm(projected[1].reshape(tok_count, heads, HD), k_gain)
    split = (images, PATCHES, heads, HD)
    queries = queries.astype(jnp.bfloat16).reshape(split)
    keys = keys.astype(jnp.bfloat16).reshape(split)
    values = projected[2].astype(jnp.bfloat16).reshape(split)
    scores = jnp.einsum(
        "iqhd,ikhd->ihqk", queries, keys, preferred_element_type=jnp.float32
    ) * HD ** (-0.5)
    scores = scores - jnp.max(scores, axis=-1, keepdims=True)
    weights = jnp.exp(scores)
    probs = (weights / jnp.sum(weights, axis=-1, keepdims=True)).astype(jnp.bfloat16)
    attended = jnp.einsum("ihqk,ikhd->iqhd", probs, values, preferred_element_type=jnp.float32)
    return attended.astype(jnp.bfloat16).reshape(tok_count, heads * HD)


def gathered(tokens, ln_gain, w_qkv, w_up, q_gain, k_gain, w_proj, w_down):
    rows = tokens.astype(jnp.float32)
    panels = lax.all_gather(tokens, "mp", axis=1, tiled=True)
    normed = layer_norm(panels.astype(jnp.float32), ln_gain).astype(jnp.bfloat16)
    projected = jnp.einsum(
        "td,dca->cta",
        normed,
        lax.all_gather(w_qkv, "fsdp", axis=0, tiled=True),
        preferred_element_type=jnp.float32,
    )
    hidden_pre = jnp.dot(
        normed,
        lax.all_gather(w_up, "fsdp", axis=0, tiled=True),
        preferred_element_type=jnp.float32,
    )
    attended = attention(projected, q_gain, k_gain)
    activated = jax.nn.gelu(hidden_pre, approximate=False).astype(jnp.bfloat16)
    joined = jnp.concatenate([attended, activated], axis=1)
    out_rows = jnp.concatenate([w_proj, w_down], axis=0)
    terms = jnp.dot(
        joined,
        lax.all_gather(out_rows, "fsdp", axis=1, tiled=True),
        preferred_element_type=jnp.float32,
    )
    branches = lax.psum_scatter(
        terms.astype(jnp.bfloat16), "mp", scatter_dimension=1, tiled=True
    ).astype(jnp.float32)
    return (rows + branches).astype(jnp.bfloat16)


def flip(z, k):
    if k == 1:
        return z + 1 - 2 * lax.rem(z, 2)
    if k == 2:
        return z + 2 - 4 * lax.div(z, 2)
    return 3 - z if k == 3 else z


def fused_kernel(
    tokens_ref, gain_ref, qgain_ref, kgain_ref, qkv_ref, up_ref, out_ref,
    terms_ref, all_qkv, all_up, all_out,
    panels, normed, projected, joined, in_tile, out_tile,
    send_sem, recv_sem, local_sem, tile_sem,
):
    me, side = lax.axis_index("fsdp"), lax.axis_index("mp")
    z, y, c = lax.div(me, 4), lax.rem(lax.div(me, 2), 2), lax.rem(me, 2)
    half = lax.rem(z, 2)
    rows = tokens_ref.shape[0]
    depth = up_ref.shape[0]
    heads = qgain_ref.shape[0] // 2
    head_cols = heads * HD
    hidden = up_ref.shape[1] // 2
    tall = 2 * rows
    width = in_tile.shape[2]

    def device(z, y, c):
        return (z * 4 + y * 2 + c, side)

    def remote(index, src, dst, target):
        return pltpu.make_async_remote_copy(
            src_ref=src,
            dst_ref=dst,
            send_sem=send_sem.at[index],
            recv_sem=recv_sem.at[index],
            device_id=target,
            device_id_type=pl.DeviceIdType.MESH,
        )

    def slot(ref, z, y, c):
        return ref.at[pl.ds(pl.multiple_of((z * 4 + y * 2 + c) * depth, depth), depth)]

    partners = [device(flip(z, k), y, c) for k in (1, 2, 3)]
    partners += [device(z, 1 - y, c), device(z, y, 1 - c), (me, 1 - side)]
    barrier = pltpu.get_barrier_semaphore()
    for partner in partners:
        pl.semaphore_signal(
            barrier, inc=1, device_id=partner, device_id_type=pl.DeviceIdType.MESH
        )
    pl.semaphore_wait(barrier, len(partners))

    wholes = (all_qkv, all_up, all_out)

    def part(t, which):
        if t == 1:
            return up_ref.at[:, pl.ds(pl.multiple_of(which * hidden, 128), hidden)]
        return (qkv_ref, None, out_ref)[t].at[which]

    copies = {}
    for t in range(3):
        base = 15 * t
        mine = slot(wholes[t], z, y, c)
        for k in range(4):
            if k:
                copies["z", t, k] = remote(
                    base + k - 1, part(t, 1 - half if k % 2 else half), mine, device(flip(z, k), y, c)
                )
            here = slot(wholes[t], flip(z, k), y, c)
            source = part(t, half) if k == 0 else here
            copies["y", t, k] = remote(base + 3 + k, source, here, device(z, 1 - y, c))
            copies["c", t, k, 0] = remote(base + 7 + k, source, here, device(z, y, 1 - c))
            across = slot(wholes[t], flip(z, k), 1 - y, c)
            copies["c", t, k, 1] = remote(base + 11 + k, across, across, device(z, y, 1 - c))
    near, far = pl.ds(0, rows), pl.ds(rows, rows)
    copies["tz"] = remote(45, tokens_ref, panels.at[side, far], device(flip(z, 1), y, c))
    copies["tx", 0] = remote(46, tokens_ref, panels.at[side, near], (me, 1 - side))
    copies["tx", 1] = remote(47, panels.at[side, far], panels.at[side, far], (me, 1 - side))

    def start(*keys):
        for key in keys:
            copies[key].start()

    def arrived(*keys):
        for key in keys:
            copies[key].wait_recv()

    def forward_z(t, k):
        arrived(("z", t, k))
        start(("y", t, k), ("c", t, k, 0))

    def forward_y(t, k):
        arrived(("y", t, k))
        start(("c", t, k, 1))

    def landed(t, k):
        arrived(("c", t, k, 0), ("c", t, k, 1))

    def stream(first, count, tiles, source, body):
        def fetch(step):
            which = lax.rem(step, 2)
            return pltpu.make_async_copy(source(step), tiles.at[which], tile_sem.at[which])

        fetch(first).start()

        def step(i, _):
            @pl.when(i + 1 < first + count)
            def _():
                fetch(i + 1).start()

            fetch(i).wait()
            body(i, tiles[lax.rem(i, 2)])
            return 0

        lax.fori_loop(first, first + count, step, 0)

    def by_rows(run, size):
        def step(i, _):
            run(pl.ds(pl.multiple_of(i * size, size), size))
            return 0

        lax.fori_loop(0, tall // size, step, 0)

    def columns(step):
        return pl.ds(pl.multiple_of(step * width, width), width)

    def project(first, count):
        def body(step, tile):
            def run(at):
                projected[at, columns(step)] = jnp.dot(
                    normed[at, :], tile, preferred_element_type=jnp.float32
                )

            by_rows(run, 512)

        stream(first, count, in_tile, lambda i: all_qkv.at[:, columns(i)], body)

    def expand(first, count):
        def body(step, tile):
            def run(at):
                pre = jnp.dot(normed[at, :], tile, preferred_element_type=jnp.float32)
                active = 0.5 * pre * (1.0 + lax.erf(pre * 0.5**0.5))
                into = pl.ds(pl.multiple_of(head_cols + step * width, width), width)
                joined[at, into] = active.astype(jnp.bfloat16)

            by_rows(run, 512)

        stream(first, count, in_tile, lambda i: all_up.at[:, columns(i)], body)

    def reduce(k):
        tile_rows = out_tile.shape[1]

        def source(i):
            begin = flip(z, k) * (4 * depth) + i * tile_rows
            return all_out.at[pl.ds(pl.multiple_of(begin, tile_rows), tile_rows)]

        def body(step, tile):
            into = pl.ds(pl.multiple_of(step * tile_rows, tile_rows), tile_rows)

            def run(at):
                terms_ref[k, at, into] = lax.dot_general(
                    joined[at, :], tile, (((1,), (1,)), ((), ())),
                    preferred_element_type=jnp.float32,
                ).astype(jnp.bfloat16)

            by_rows(run, 512)

        stream(0, 4 * depth // tile_rows, out_tile, source, body)

    def attend(first, count):
        def step(i, _):
            image, head = lax.div(i, heads), lax.rem(i, heads)
            at = pl.ds(pl.multiple_of(image * PATCHES, PATCHES), PATCHES)

            def pick(group):
                begin = pl.multiple_of(group * head_cols + head * HD, HD)
                return projected[at, pl.ds(begin, HD)]

            one = pl.ds(half * heads + head, 1)
            queries = layer_norm(pick(0), qgain_ref[one, :]).astype(jnp.bfloat16)
            keys = layer_norm(pick(1), kgain_ref[one, :]).astype(jnp.bfloat16)
            values = pick(2).astype(jnp.bfloat16)
            scores = lax.dot_general(
                queries, keys, (((1,), (1,)), ((), ())), preferred_element_type=jnp.float32
            ) * HD ** (-0.5)
            weights = jnp.exp(scores - jnp.max(scores, axis=-1, keepdims=True))
            probs = weights / jnp.sum(weights, axis=-1, keepdims=True)
            mixed = jnp.dot(
                probs.astype(jnp.bfloat16), values, preferred_element_type=jnp.float32
            )
            joined[at, pl.ds(pl.multiple_of(head * HD, HD), HD)] = mixed.astype(jnp.bfloat16)
            return 0

        lax.fori_loop(first, first + count, step, 0)

    def normalise():
        def run(at):
            left = panels[0, at, :].astype(jnp.float32)
            right = panels[1, at, :].astype(jnp.float32)
            total = jnp.sum(left, axis=-1, keepdims=True) + jnp.sum(right, axis=-1, keepdims=True)
            cols = panels.shape[2]
            mean = total / (2 * cols)
            left, right = left - mean, right - mean
            square = jnp.sum(left * left, axis=-1, keepdims=True)
            square = square + jnp.sum(right * right, axis=-1, keepdims=True)
            scale = lax.rsqrt(square / (2 * cols) + 1e-06)
            normed[at, :cols] = (left * scale * gain_ref[:, :cols]).astype(jnp.bfloat16)
            normed[at, cols:] = (right * scale * gain_ref[:, cols:]).astype(jnp.bfloat16)

        by_rows(run, 64)

    locals_ = [
        pltpu.make_async_copy(part(t, half), slot(wholes[t], z, y, c), local_sem.at[t])
        for t in range(3)
    ]
    locals_.append(
        pltpu.make_async_copy(tokens_ref, panels.at[side, near], local_sem.at[3])
    )

    qkv_steps, up_steps = 3 * head_cols // width, hidden // width
    tiles_of_heads = heads * (tall // PATCHES)

    start("tz", ("tx", 0), ("z", 0, 1), ("z", 0, 2), ("z", 0, 3))
    start(("y", 0, 0), ("c", 0, 0, 0), ("y", 1, 0), ("y", 2, 0), ("c", 1, 0, 0), ("c", 2, 0, 0))
    for copy in locals_:
        copy.start()
    arrived("tz")
    start(("tx", 1))
    forward_y(0, 0)
    for k in (1, 2, 3):
        forward_z(0, k)
    start(("z", 1, 1), ("z", 1, 2))
    for copy in locals_:
        copy.wait()
    arrived(("tx", 0), ("tx", 1))
    normalise()
    forward_y(1, 0)
    forward_y(2, 0)
    for k in (1, 2):
        forward_z(1, k)
    start(("z", 1, 3), ("z", 2, 1))
    for k in (1, 2, 3):
        forward_y(0, k)
    for k in range(4):
        landed(0, k)
    project(0, qkv_steps)
    attend(0, tiles_of_heads // 2)
    forward_z(1, 3)
    start(("z", 2, 2))
    forward_z(2, 1)
    forward_y(1, 1)
    forward_y(1, 2)
    attend(tiles_of_heads // 2, tiles_of_heads - tiles_of_heads // 2)
    forward_y(1, 3)
    for k in range(4):
        landed(1, k)
    expand(0, up_steps // 2)
    forward_z(2, 2)
    start(("z", 2, 3))
    forward_y(2, 1)
    expand(up_steps // 2, up_steps - up_steps // 2)
    for k in (0, 1):
        landed(2, k)
        reduce(k)
    forward_y(2, 2)
    landed(2, 2)
    reduce(2)
    forward_z(2, 3)
    forward_y(2, 3)
    landed(2, 3)
    reduce(3)
    for copy in copies.values():
        copy.wait_send()


def fused(tokens, ln_gain, w_qkv, w_up, q_gain, k_gain, w_proj, w_down):
    side = lax.axis_index("mp")
    me = lax.axis_index("fsdp")
    z = me // 4
    half = z % 2
    rows, cols = tokens.shape
    depth = w_up.shape[0]
    heads = q_gain.shape[0] // 2
    head_cols, hidden = heads * HD, w_up.shape[1] // 2
    tall, whole, joint = 2 * rows, 16 * depth, head_cols + hidden
    qkv = w_qkv.reshape(depth, 3, 2, head_cols).transpose(2, 0, 1, 3)
    qkv = qkv.reshape(2, depth, 3 * head_cols)
    outs = jnp.concatenate(
        [w_proj.reshape(2, head_cols, depth), w_down.reshape(2, hidden, depth)], axis=1
    ).transpose(0, 2, 1)
    bf16, f32 = jnp.bfloat16, jnp.float32
    anywhere, vmem = pl.BlockSpec(memory_space=pl.ANY), pl.BlockSpec(memory_space=pltpu.VMEM)
    terms = pl.pallas_call(
        fused_kernel,
        out_shape=[
            jax.ShapeDtypeStruct((4, tall, 4 * depth), bf16),
            jax.ShapeDtypeStruct((whole, 3 * head_cols), bf16),
            jax.ShapeDtypeStruct((whole, hidden), bf16),
            jax.ShapeDtypeStruct((whole, joint), bf16),
        ],
        in_specs=[anywhere, vmem, vmem, vmem, anywhere, anywhere, anywhere],
        out_specs=[vmem, anywhere, anywhere, anywhere],
        scratch_shapes=[
            pltpu.VMEM((2, tall, cols), bf16),
            pltpu.VMEM((tall, 2 * cols), bf16),
            pltpu.VMEM((tall, 3 * head_cols), f32),
            pltpu.VMEM((tall, joint), bf16),
            pltpu.VMEM((2, whole, 256), bf16),
            pltpu.VMEM((2, 256, joint), bf16),
            pltpu.SemaphoreType.DMA((48,)),
            pltpu.SemaphoreType.DMA((48,)),
            pltpu.SemaphoreType.DMA((4,)),
            pltpu.SemaphoreType.DMA((2,)),
        ],
        compiler_params=pltpu.CompilerParams(
            collective_id=0, has_side_effects=True, vmem_limit_bytes=58 * 2**20
        ),
    )(tokens, ln_gain[None], q_gain, k_gain, qkv, w_up, outs)[0]

    def swap(value, mask, axis="fsdp"):
        count = 16 if axis == "fsdp" else 2
        return lax.ppermute(value, axis, [(i, i ^ mask) for i in range(count)])

    keep_low = z // 2 == side
    own, far = [], []
    for stage in range(2):
        low, high = terms[stage], terms[stage + 2]
        keep = jnp.where(keep_low, low, high)
        got = swap(jnp.where(keep_low, high, low), 1, "mp")
        total = keep.astype(f32) + got.astype(f32)
        own.append(total[:rows])
        far.append(swap(total[rows:].astype(bf16), 4))
    done = [own[s] + far[1 - s].astype(f32) for s in range(2)]
    branches = jnp.where(
        half == 0, jnp.concatenate(done, axis=1), jnp.concatenate(done[::-1], axis=1)
    )
    return (tokens.astype(f32) + branches).astype(bf16)


def solution(mesh):
    n, sides = mesh.shape["fsdp"], mesh.shape["mp"]
    return jax.shard_map(
        fused if (n, sides) == (16, 2) else gathered,
        mesh=mesh,
        in_specs=(
            P("fsdp", "mp"),
            P(),
            P("fsdp", None, "mp"),
            P("fsdp", "mp"),
            P("mp", None),
            P("mp", None),
            P("mp", "fsdp"),
            P("mp", "fsdp"),
        ),
        out_specs=P("fsdp", "mp"),
        check_vma=False,
    )
```

```python
import jax
import jax.numpy as jnp
from jax import lax
from jax.experimental import pallas as pl
from jax.experimental.pallas import tpu as pltpu
from jax.sharding import PartitionSpec as P

HD = 128
PATCHES = 256
LAST_PIECES = 3
SEMAPHORES = 80


def layer_norm(values, gain):
    mean = jnp.mean(values, axis=-1, keepdims=True)
    centred = values - mean
    variance = jnp.mean(centred * centred, axis=-1, keepdims=True)
    return centred * lax.rsqrt(variance + 1e-06) * gain


def attention(projected, q_gain, k_gain):
    tok_count = projected[0].shape[0]
    heads = q_gain.shape[0]
    images = tok_count // PATCHES
    queries = layer_norm(projected[0].reshape(tok_count, heads, HD), q_gain)
    keys = layer_norm(projected[1].reshape(tok_count, heads, HD), k_gain)
    split = (images, PATCHES, heads, HD)
    queries = queries.astype(jnp.bfloat16).reshape(split)
    keys = keys.astype(jnp.bfloat16).reshape(split)
    values = projected[2].astype(jnp.bfloat16).reshape(split)
    scores = jnp.einsum(
        "iqhd,ikhd->ihqk", queries, keys, preferred_element_type=jnp.float32
    ) * HD ** (-0.5)
    scores = scores - jnp.max(scores, axis=-1, keepdims=True)
    weights = jnp.exp(scores)
    probs = (weights / jnp.sum(weights, axis=-1, keepdims=True)).astype(jnp.bfloat16)
    attended = jnp.einsum("ihqk,ikhd->iqhd", probs, values, preferred_element_type=jnp.float32)
    return attended.astype(jnp.bfloat16).reshape(tok_count, heads * HD)


def gathered(tokens, ln_gain, w_qkv, w_up, q_gain, k_gain, w_proj, w_down):
    rows = tokens.astype(jnp.float32)
    panels = lax.all_gather(tokens, "mp", axis=1, tiled=True)
    normed = layer_norm(panels.astype(jnp.float32), ln_gain).astype(jnp.bfloat16)
    projected = jnp.einsum(
        "td,dca->cta",
        normed,
        lax.all_gather(w_qkv, "fsdp", axis=0, tiled=True),
        preferred_element_type=jnp.float32,
    )
    hidden_pre = jnp.dot(
        normed,
        lax.all_gather(w_up, "fsdp", axis=0, tiled=True),
        preferred_element_type=jnp.float32,
    )
    attended = attention(projected, q_gain, k_gain)
    activated = jax.nn.gelu(hidden_pre, approximate=False).astype(jnp.bfloat16)
    joined = jnp.concatenate([attended, activated], axis=1)
    out_rows = jnp.concatenate([w_proj, w_down], axis=0)
    terms = jnp.dot(
        joined,
        lax.all_gather(out_rows, "fsdp", axis=1, tiled=True),
        preferred_element_type=jnp.float32,
    )
    branches = lax.psum_scatter(
        terms.astype(jnp.bfloat16), "mp", scatter_dimension=1, tiled=True
    ).astype(jnp.float32)
    return (rows + branches).astype(jnp.bfloat16)


def flip(z, k):
    if k == 1:
        return z + 1 - 2 * lax.rem(z, 2)
    if k == 2:
        return z + 2 - 4 * lax.div(z, 2)
    return 3 - z if k == 3 else z


def fused_kernel(
    tokens_ref, gain_ref, qgain_ref, kgain_ref, q_ref, k_ref, v_ref, up_ref, outs_ref,
    block_ref, all_qkv, all_up, all_out,
    panels, normed, projected, joined, in_tile, out_tile, terms_ref, crossed, passed, summed,
    send_sem, recv_sem, local_sem, tile_sem,
):
    me, side = lax.axis_index("fsdp"), lax.axis_index("mp")
    z, y, c = lax.div(me, 4), lax.rem(lax.div(me, 2), 2), lax.rem(me, 2)
    half = lax.rem(z, 2)
    rows = tokens_ref.shape[0]
    depth = up_ref.shape[0]
    heads = qgain_ref.shape[0] // 2
    head_cols = heads * HD
    hidden = up_ref.shape[1] // 2
    tall = 2 * rows
    width = in_tile.shape[2]

    def device(z, y, c):
        return (z * 4 + y * 2 + c, side)

    def remote(index, src, dst, target):
        return pltpu.make_async_remote_copy(
            src_ref=src,
            dst_ref=dst,
            send_sem=send_sem.at[index],
            recv_sem=recv_sem.at[index],
            device_id=target,
            device_id_type=pl.DeviceIdType.MESH,
        )

    def slot(t, z, y, c, piece=0, pieces=1):
        size = depth // pieces
        begin = (z * 4 + y * 2 + c) * depth + piece * size
        return wholes[t].at[pl.ds(pl.multiple_of(begin, size), size)]

    wholes = (all_qkv, all_up, all_out)
    partners = [device(flip(z, k), y, c) for k in (1, 2, 3)]
    partners += [device(z, 1 - y, c), device(z, y, 1 - c), (me, 1 - side)]
    barrier = pltpu.get_barrier_semaphore()
    for partner in partners:
        pl.semaphore_signal(
            barrier, inc=1, device_id=partner, device_id_type=pl.DeviceIdType.MESH
        )
    pl.semaphore_wait(barrier, len(partners))

    def pieces_of(t, k):
        return LAST_PIECES if (t, k) == (2, 3) else 1

    def part(t, which, piece=0, pieces=1):
        if t == 1:
            return up_ref.at[:, pl.ds(pl.multiple_of(which * hidden, 128), hidden)]
        size = depth // pieces
        return outs_ref.at[which, pl.ds(piece * size, size)]

    def thirds(which, into):
        cols = pl.ds(pl.multiple_of(which * head_cols, 128), head_cols)
        for g, ref in enumerate((q_ref, k_ref, v_ref)):
            yield g, ref.at[:, cols], into.at[:, pl.ds(g * head_cols, head_cols)]

    copies = {}

    def add(key, src, dst, target):
        copies[key] = remote(len(copies), src, dst, target)

    for t in range(3):
        for k in range(4):
            target = device(flip(z, k), y, c)
            which = 1 - half if k % 2 else half
            count = pieces_of(t, k)
            if k and t == 0:
                for g, src, dst in thirds(which, slot(0, z, y, c)):
                    add(("z", t, k, g), src, dst, target)
            for p in range(count):
                if k and t:
                    add(("z", t, k, p), part(t, which, p, count), slot(t, z, y, c, p, count), target)
                here = slot(t, flip(z, k), y, c, p, count)
                source = part(t, half) if k == 0 and t else here
                add(("y", t, k, p), source, here, device(z, 1 - y, c))
                add(("c", t, k, p, 0), source, here, device(z, y, 1 - c))
                across = slot(t, flip(z, k), 1 - y, c, p, count)
                add(("c", t, k, p, 1), across, across, device(z, y, 1 - c))
    near, far = pl.ds(0, rows), pl.ds(rows, rows)
    beside, below = (me, 1 - side), device(flip(z, 1), y, c)
    add("tz", tokens_ref, panels.at[side, far], below)
    add(("tx", 0), tokens_ref, panels.at[side, near], beside)
    add(("tx", 1), panels.at[side, far], panels.at[side, far], beside)
    high = lax.div(z, 2)
    keep_low = 1 - high - side + 2 * high * side
    for s in range(2):
        for r, at in ((0, near), (1, far)):
            add(("ox", s, r), terms_ref.at[s + 2 * keep_low, at], crossed.at[s, at], beside)
        add(("oz", s), summed.at[s], passed.at[s], below)
    assert len(copies) <= SEMAPHORES

    def start(*keys):
        for key in keys:
            copies[key].start()

    def arrived(*keys):
        for key in keys:
            copies[key].wait_recv()

    def start_z(t, k):
        start(*[key for key in copies if key[:3] == ("z", t, k)])

    def forward_z(t, k, p=0):
        arrived(*[("z", t, k, g) for g in range(3)] if t == 0 else [("z", t, k, p)])
        start(("y", t, k, p), ("c", t, k, p, 0))

    def forward_y(t, k, p=0):
        arrived(("y", t, k, p))
        start(("c", t, k, p, 1))

    def landed(t, k):
        for p in range(pieces_of(t, k)):
            arrived(("c", t, k, p, 0), ("c", t, k, p, 1))

    def stream(first, count, tiles, source, body):
        def fetch(step):
            which = lax.rem(step, 2)
            return pltpu.make_async_copy(source(step), tiles.at[which], tile_sem.at[which])

        fetch(first).start()

        def step(i, _):
            @pl.when(i + 1 < first + count)
            def _():
                fetch(i + 1).start()

            fetch(i).wait()
            body(i, tiles[lax.rem(i, 2)])
            return 0

        lax.fori_loop(first, first + count, step, 0)

    def by_rows(run, size):
        def step(i, _):
            run(pl.ds(pl.multiple_of(i * size, size), size))
            return 0

        lax.fori_loop(0, tall // size, step, 0)

    def columns(step):
        return pl.ds(pl.multiple_of(step * width, width), width)

    def project(first, count):
        def body(step, tile):
            def run(at):
                projected[at, columns(step)] = jnp.dot(
                    normed[at, :], tile, preferred_element_type=jnp.float32
                )

            by_rows(run, 512)

        stream(first, count, in_tile, lambda i: all_qkv.at[:, columns(i)], body)

    def expand(first, count):
        def body(step, tile):
            def run(at):
                pre = jnp.dot(normed[at, :], tile, preferred_element_type=jnp.float32)
                active = 0.5 * pre * (1.0 + lax.erf(pre * 0.5**0.5))
                into = pl.ds(pl.multiple_of(head_cols + step * width, width), width)
                joined[at, into] = active.astype(jnp.bfloat16)

            by_rows(run, 512)

        stream(first, count, in_tile, lambda i: all_up.at[:, columns(i)], body)

    def reduce(k, halves=(0, 1)):
        tile_rows = out_tile.shape[1]

        def source(i):
            begin = flip(z, k) * (4 * depth) + i * tile_rows
            return all_out.at[pl.ds(pl.multiple_of(begin, tile_rows), tile_rows)]

        def body(step, tile):
            into = pl.ds(pl.multiple_of(step * tile_rows, tile_rows), tile_rows)
            for r in halves:
                at = (near, far)[r]
                terms_ref[k, at, into] = lax.dot_general(
                    joined[at, :], tile, (((1,), (1,)), ((), ())),
                    preferred_element_type=jnp.float32,
                ).astype(jnp.bfloat16)

        stream(0, 4 * depth // tile_rows, out_tile, source, body)

    def own_sum(s, at):
        kept = terms_ref[s + 2 * (1 - keep_low), at, :].astype(jnp.float32)
        return kept + crossed[s, at, :].astype(jnp.float32)

    def pass_on(s):
        arrived(("ox", s, 1))

        def step(i, _):
            begin = pl.multiple_of(i * 128, 128)
            total = own_sum(s, pl.ds(rows + begin, 128))
            summed[s, pl.ds(begin, 128), :] = total.astype(jnp.bfloat16)
            return 0

        lax.fori_loop(0, rows // 128, step, 0)
        start(("oz", s))

    def finish(s):
        size = 4 * depth
        place = half + s - 2 * half * s

        def step(i, _):
            at = pl.ds(pl.multiple_of(i * 128, 128), 128)
            cols = pl.ds(pl.multiple_of(place * size, 128), size)
            total = own_sum(s, at) + passed[1 - s, at, :].astype(jnp.float32)
            total = panels[side, at, cols].astype(jnp.float32) + total
            block_ref[at, cols] = total.astype(jnp.bfloat16)
            return 0

        lax.fori_loop(0, rows // 128, step, 0)

    def attend(first, count):
        def step(i, _):
            image, head = lax.div(i, heads), lax.rem(i, heads)
            at = pl.ds(pl.multiple_of(image * PATCHES, PATCHES), PATCHES)

            def pick(group):
                begin = pl.multiple_of(group * head_cols + head * HD, HD)
                return projected[at, pl.ds(begin, HD)]

            one = pl.ds(half * heads + head, 1)
            queries = layer_norm(pick(0), qgain_ref[one, :]).astype(jnp.bfloat16)
            keys = layer_norm(pick(1), kgain_ref[one, :]).astype(jnp.bfloat16)
            values = pick(2).astype(jnp.bfloat16)
            scores = lax.dot_general(
                queries, keys, (((1,), (1,)), ((), ())), preferred_element_type=jnp.float32
            ) * HD ** (-0.5)
            weights = jnp.exp(scores - jnp.max(scores, axis=-1, keepdims=True))
            probs = weights / jnp.sum(weights, axis=-1, keepdims=True)
            mixed = jnp.dot(
                probs.astype(jnp.bfloat16), values, preferred_element_type=jnp.float32
            )
            joined[at, pl.ds(pl.multiple_of(head * HD, HD), HD)] = mixed.astype(jnp.bfloat16)
            return 0

        lax.fori_loop(first, first + count, step, 0)

    def normalise():
        def run(at):
            left = panels[0, at, :].astype(jnp.float32)
            right = panels[1, at, :].astype(jnp.float32)
            total = jnp.sum(left, axis=-1, keepdims=True) + jnp.sum(right, axis=-1, keepdims=True)
            cols = panels.shape[2]
            mean = total / (2 * cols)
            left, right = left - mean, right - mean
            square = jnp.sum(left * left, axis=-1, keepdims=True)
            square = square + jnp.sum(right * right, axis=-1, keepdims=True)
            scale = lax.rsqrt(square / (2 * cols) + 1e-06)
            normed[at, :cols] = (left * scale * gain_ref[:, :cols]).astype(jnp.bfloat16)
            normed[at, cols:] = (right * scale * gain_ref[:, cols:]).astype(jnp.bfloat16)

        by_rows(run, 64)

    own = [pltpu.make_async_copy(tokens_ref, panels.at[side, near], local_sem.at[0])]
    for t in (1, 2):
        own.append(pltpu.make_async_copy(part(t, half), slot(t, z, y, c), local_sem.at[t]))
    first = [
        pltpu.make_async_copy(src, dst, local_sem.at[3 + g])
        for g, src, dst in thirds(half, slot(0, z, y, c))
    ]

    qkv_steps, up_steps = 3 * head_cols // width, hidden // width
    quarter = heads * (tall // PATCHES) // 4

    for k in (1, 2, 3):
        start_z(0, k)
    start("tz", ("tx", 0))
    for copy in first + own:
        copy.start()
    for copy in first:
        copy.wait()
    for t in range(3):
        start(("y", t, 0, 0), ("c", t, 0, 0, 0))
    arrived("tz")
    start(("tx", 1))
    forward_y(0, 0)
    forward_z(0, 1)
    forward_z(0, 2)
    start_z(1, 1)
    start_z(1, 2)
    forward_z(0, 3)
    for copy in own:
        copy.wait()
    arrived(("tx", 0), ("tx", 1))
    normalise()
    forward_y(1, 0)
    forward_y(2, 0)
    forward_z(1, 1)
    forward_z(1, 2)
    start_z(1, 3)
    start_z(2, 1)
    for k in (1, 2, 3):
        forward_y(0, k)
    for k in range(4):
        landed(0, k)
    project(0, qkv_steps)
    attend(0, quarter)
    forward_z(1, 3)
    start_z(2, 2)
    forward_z(2, 1)
    forward_y(1, 1)
    forward_y(1, 2)
    attend(quarter, 3 * quarter)
    forward_y(1, 3)
    for k in range(4):
        landed(1, k)
    expand(0, up_steps // 2)
    forward_z(2, 2)
    start(("z", 2, 3, 0), ("z", 2, 3, 1))
    forward_y(2, 1)
    expand(up_steps // 2, up_steps - up_steps // 2)
    landed(2, 0)
    reduce(0)
    forward_y(2, 2)
    landed(2, 2)
    reduce(2)
    start(("ox", 0, 1), ("ox", 0, 0))
    forward_z(2, 3, 0)
    for p in range(2, LAST_PIECES):
        start(("z", 2, 3, p))
    landed(2, 1)
    reduce(1)
    for p in range(1, LAST_PIECES):
        forward_z(2, 3, p)
    pass_on(0)
    for p in range(LAST_PIECES):
        forward_y(2, 3, p)
    landed(2, 3)
    reduce(3, (1,))
    start(("ox", 1, 1))
    reduce(3, (0,))
    start(("ox", 1, 0))
    arrived(("ox", 0, 0), ("oz", 0))
    pass_on(1)
    arrived(("ox", 1, 0))
    finish(1)
    arrived(("oz", 1))
    finish(0)
    for copy in copies.values():
        copy.wait_send()


def fused(tokens, ln_gain, w_qkv, w_up, q_gain, k_gain, w_proj, w_down):
    rows, cols = tokens.shape
    depth = w_up.shape[0]
    heads = q_gain.shape[0] // 2
    head_cols, hidden = heads * HD, w_up.shape[1] // 2
    tall, whole, joint = 2 * rows, 16 * depth, head_cols + hidden
    outs = jnp.concatenate(
        [w_proj.reshape(2, head_cols, depth), w_down.reshape(2, hidden, depth)], axis=1
    ).transpose(0, 2, 1)
    bf16, f32 = jnp.bfloat16, jnp.float32
    anywhere, vmem = pl.BlockSpec(memory_space=pl.ANY), pl.BlockSpec(memory_space=pltpu.VMEM)
    return pl.pallas_call(
        fused_kernel,
        out_shape=[
            jax.ShapeDtypeStruct((rows, cols), bf16),
            jax.ShapeDtypeStruct((whole, 3 * head_cols), bf16),
            jax.ShapeDtypeStruct((whole, hidden), bf16),
            jax.ShapeDtypeStruct((whole, joint), bf16),
        ],
        in_specs=[anywhere, vmem, vmem, vmem] + [anywhere] * 5,
        out_specs=[vmem, anywhere, anywhere, anywhere],
        scratch_shapes=[
            pltpu.VMEM((2, tall, cols), bf16),
            pltpu.VMEM((tall, 2 * cols), bf16),
            pltpu.VMEM((tall, 3 * head_cols), f32),
            pltpu.VMEM((tall, joint), bf16),
            pltpu.VMEM((2, whole, 256), bf16),
            pltpu.VMEM((2, 256, joint), bf16),
            pltpu.VMEM((4, tall, 4 * depth), bf16),
            pltpu.VMEM((2, tall, 4 * depth), bf16),
            pltpu.VMEM((2, rows, 4 * depth), bf16),
            pltpu.VMEM((2, rows, 4 * depth), bf16),
            pltpu.SemaphoreType.DMA((SEMAPHORES,)),
            pltpu.SemaphoreType.DMA((SEMAPHORES,)),
            pltpu.SemaphoreType.DMA((6,)),
            pltpu.SemaphoreType.DMA((2,)),
        ],
        compiler_params=pltpu.CompilerParams(
            collective_id=0, has_side_effects=True, vmem_limit_bytes=58 * 2**20
        ),
    )(
        tokens, ln_gain[None], q_gain, k_gain,
        w_qkv[:, 0], w_qkv[:, 1], w_qkv[:, 2], w_up, outs,
    )[0]


def solution(mesh):
    n, sides = mesh.shape["fsdp"], mesh.shape["mp"]
    return jax.shard_map(
        fused if (n, sides) == (16, 2) else gathered,
        mesh=mesh,
        in_specs=(
            P("fsdp", "mp"),
            P(),
            P("fsdp", None, "mp"),
            P("fsdp", "mp"),
            P("mp", None),
            P("mp", None),
            P("mp", "fsdp"),
            P("mp", "fsdp"),
        ),
        out_specs=P("fsdp", "mp"),
        check_vma=False,
    )
```

```python
import jax
import jax.numpy as jnp
from jax import lax
from jax.experimental import pallas as pl
from jax.experimental.pallas import tpu as pltpu
from jax.sharding import PartitionSpec as P

HD = 128
PATCHES = 256
LAST_PIECES = 3
SEMAPHORES = 80


def layer_norm(values, gain):
    mean = jnp.mean(values, axis=-1, keepdims=True)
    centred = values - mean
    variance = jnp.mean(centred * centred, axis=-1, keepdims=True)
    return centred * lax.rsqrt(variance + 1e-06) * gain


def attention(projected, q_gain, k_gain):
    tok_count = projected[0].shape[0]
    heads = q_gain.shape[0]
    images = tok_count // PATCHES
    queries = layer_norm(projected[0].reshape(tok_count, heads, HD), q_gain)
    keys = layer_norm(projected[1].reshape(tok_count, heads, HD), k_gain)
    split = (images, PATCHES, heads, HD)
    queries = queries.astype(jnp.bfloat16).reshape(split)
    keys = keys.astype(jnp.bfloat16).reshape(split)
    values = projected[2].astype(jnp.bfloat16).reshape(split)
    scores = jnp.einsum(
        "iqhd,ikhd->ihqk", queries, keys, preferred_element_type=jnp.float32
    ) * HD ** (-0.5)
    scores = scores - jnp.max(scores, axis=-1, keepdims=True)
    weights = jnp.exp(scores)
    probs = (weights / jnp.sum(weights, axis=-1, keepdims=True)).astype(jnp.bfloat16)
    attended = jnp.einsum("ihqk,ikhd->iqhd", probs, values, preferred_element_type=jnp.float32)
    return attended.astype(jnp.bfloat16).reshape(tok_count, heads * HD)


def gathered(tokens, ln_gain, w_qkv, w_up, q_gain, k_gain, w_proj, w_down):
    rows = tokens.astype(jnp.float32)
    panels = lax.all_gather(tokens, "mp", axis=1, tiled=True)
    normed = layer_norm(panels.astype(jnp.float32), ln_gain).astype(jnp.bfloat16)
    projected = jnp.einsum(
        "td,dca->cta",
        normed,
        lax.all_gather(w_qkv, "fsdp", axis=0, tiled=True),
        preferred_element_type=jnp.float32,
    )
    hidden_pre = jnp.dot(
        normed,
        lax.all_gather(w_up, "fsdp", axis=0, tiled=True),
        preferred_element_type=jnp.float32,
    )
    attended = attention(projected, q_gain, k_gain)
    activated = jax.nn.gelu(hidden_pre, approximate=False).astype(jnp.bfloat16)
    joined = jnp.concatenate([attended, activated], axis=1)
    out_rows = jnp.concatenate([w_proj, w_down], axis=0)
    terms = jnp.dot(
        joined,
        lax.all_gather(out_rows, "fsdp", axis=1, tiled=True),
        preferred_element_type=jnp.float32,
    )
    branches = lax.psum_scatter(
        terms.astype(jnp.bfloat16), "mp", scatter_dimension=1, tiled=True
    ).astype(jnp.float32)
    return (rows + branches).astype(jnp.bfloat16)


def flip(z, k):
    if k == 1:
        return z + 1 - 2 * lax.rem(z, 2)
    if k == 2:
        return z + 2 - 4 * lax.div(z, 2)
    return 3 - z if k == 3 else z


def fused_kernel(
    tokens_ref, gain_ref, qgain_ref, kgain_ref, q_ref, k_ref, v_ref, up_ref, outs_ref,
    block_ref, all_qkv, all_up, all_out,
    panels, normed, projected, joined, in_tile, out_tile, terms_ref, crossed, passed, summed,
    send_sem, recv_sem, local_sem, tile_sem,
):
    me, side = lax.axis_index("fsdp"), lax.axis_index("mp")
    z, y, c = lax.div(me, 4), lax.rem(lax.div(me, 2), 2), lax.rem(me, 2)
    half = lax.rem(z, 2)
    rows = tokens_ref.shape[0]
    depth = up_ref.shape[0]
    heads = qgain_ref.shape[0] // 2
    head_cols = heads * HD
    hidden = up_ref.shape[1] // 2
    tall = 2 * rows
    width = in_tile.shape[2]

    def device(z, y, c):
        return (z * 4 + y * 2 + c, side)

    def remote(index, src, dst, target):
        return pltpu.make_async_remote_copy(
            src_ref=src,
            dst_ref=dst,
            send_sem=send_sem.at[index],
            recv_sem=recv_sem.at[index],
            device_id=target,
            device_id_type=pl.DeviceIdType.MESH,
        )

    def slot(t, z, y, c, piece=0, pieces=1):
        size = depth // pieces
        begin = (z * 4 + y * 2 + c) * depth + piece * size
        return wholes[t].at[pl.ds(pl.multiple_of(begin, size), size)]

    wholes = (all_qkv, all_up, all_out)
    partners = [device(flip(z, k), y, c) for k in (1, 2, 3)]
    partners += [device(z, 1 - y, c), device(z, y, 1 - c), (me, 1 - side)]
    barrier = pltpu.get_barrier_semaphore()
    for partner in partners:
        pl.semaphore_signal(
            barrier, inc=1, device_id=partner, device_id_type=pl.DeviceIdType.MESH
        )
    pl.semaphore_wait(barrier, len(partners))

    def pieces_of(t, k):
        return LAST_PIECES if (t, k) == (2, 3) else 1

    def part(t, which, piece=0, pieces=1):
        if t == 1:
            return up_ref.at[:, pl.ds(pl.multiple_of(which * hidden, 128), hidden)]
        size = depth // pieces
        return outs_ref.at[which, pl.ds(piece * size, size)]

    def thirds(which, into):
        cols = pl.ds(pl.multiple_of(which * head_cols, 128), head_cols)
        for g, ref in enumerate((q_ref, k_ref, v_ref)):
            yield g, ref.at[:, cols], into.at[:, pl.ds(g * head_cols, head_cols)]

    copies = {}

    def add(key, src, dst, target):
        copies[key] = remote(len(copies), src, dst, target)

    for t in range(3):
        for k in range(4):
            target = device(flip(z, k), y, c)
            which = 1 - half if k % 2 else half
            count = pieces_of(t, k)
            if k and t == 0:
                for g, src, dst in thirds(which, slot(0, z, y, c)):
                    add(("z", t, k, g), src, dst, target)
            for p in range(count):
                if k and t:
                    add(("z", t, k, p), part(t, which, p, count), slot(t, z, y, c, p, count), target)
                here = slot(t, flip(z, k), y, c, p, count)
                source = part(t, half) if k == 0 and t else here
                add(("y", t, k, p), source, here, device(z, 1 - y, c))
                add(("c", t, k, p, 0), source, here, device(z, y, 1 - c))
                across = slot(t, flip(z, k), 1 - y, c, p, count)
                add(("c", t, k, p, 1), across, across, device(z, y, 1 - c))
    near, far = pl.ds(0, rows), pl.ds(rows, rows)
    beside, below = (me, 1 - side), device(flip(z, 1), y, c)
    add("tz", tokens_ref, panels.at[side, far], below)
    add(("tx", 0), tokens_ref, panels.at[side, near], beside)
    add(("tx", 1), panels.at[side, far], panels.at[side, far], beside)
    high = lax.div(z, 2)
    keep_low = 1 - high - side + 2 * high * side
    for s in range(2):
        for r, at in ((0, near), (1, far)):
            add(("ox", s, r), terms_ref.at[s + 2 * keep_low, at], crossed.at[s, at], beside)
        add(("oz", s), summed.at[s], passed.at[s], below)
    assert len(copies) <= SEMAPHORES

    def start(*keys):
        for key in keys:
            copies[key].start()

    def arrived(*keys):
        for key in keys:
            copies[key].wait_recv()

    def start_z(t, k):
        start(*[key for key in copies if key[:3] == ("z", t, k)])

    def forward_z(t, k, p=0):
        arrived(*[("z", t, k, g) for g in range(3)] if t == 0 else [("z", t, k, p)])
        start(("y", t, k, p), ("c", t, k, p, 0))

    def forward_y(t, k, p=0):
        arrived(("y", t, k, p))
        start(("c", t, k, p, 1))

    def landed(t, k):
        for p in range(pieces_of(t, k)):
            arrived(("c", t, k, p, 0), ("c", t, k, p, 1))

    def stream(first, count, tiles, source, body):
        def fetch(step):
            which = lax.rem(step, 2)
            return pltpu.make_async_copy(source(step), tiles.at[which], tile_sem.at[which])

        fetch(first).start()

        def step(i, _):
            @pl.when(i + 1 < first + count)
            def _():
                fetch(i + 1).start()

            fetch(i).wait()
            body(i, tiles[lax.rem(i, 2)])
            return 0

        lax.fori_loop(first, first + count, step, 0)

    def by_rows(run, size):
        def step(i, _):
            run(pl.ds(pl.multiple_of(i * size, size), size))
            return 0

        lax.fori_loop(0, tall // size, step, 0)

    def columns(step):
        return pl.ds(pl.multiple_of(step * width, width), width)

    def project(first, count):
        def body(step, tile):
            def run(at):
                projected[at, columns(step)] = jnp.dot(
                    normed[at, :], tile, preferred_element_type=jnp.float32
                )

            by_rows(run, 512)

        stream(first, count, in_tile, lambda i: all_qkv.at[:, columns(i)], body)

    def expand(first, count):
        def body(step, tile):
            def run(at):
                pre = jnp.dot(normed[at, :], tile, preferred_element_type=jnp.float32)
                active = 0.5 * pre * (1.0 + lax.erf(pre * 0.5**0.5))
                into = pl.ds(pl.multiple_of(head_cols + step * width, width), width)
                joined[at, into] = active.astype(jnp.bfloat16)

            run(near)
            run(far)

        stream(first, count, in_tile, lambda i: all_up.at[:, columns(i)], body)

    def reduce(k, halves=(0, 1)):
        tile_rows = out_tile.shape[1]

        def source(i):
            begin = flip(z, k) * (4 * depth) + i * tile_rows
            return all_out.at[pl.ds(pl.multiple_of(begin, tile_rows), tile_rows)]

        def body(step, tile):
            into = pl.ds(pl.multiple_of(step * tile_rows, tile_rows), tile_rows)
            for r in halves:
                at = (near, far)[r]
                terms_ref[k, at, into] = lax.dot_general(
                    joined[at, :], tile, (((1,), (1,)), ((), ())),
                    preferred_element_type=jnp.float32,
                ).astype(jnp.bfloat16)

        stream(0, 4 * depth // tile_rows, out_tile, source, body)

    def own_sum(s, at):
        kept = terms_ref[s + 2 * (1 - keep_low), at, :].astype(jnp.float32)
        return kept + crossed[s, at, :].astype(jnp.float32)

    def pass_on(s):
        arrived(("ox", s, 1))

        def step(i, _):
            begin = pl.multiple_of(i * 128, 128)
            total = own_sum(s, pl.ds(rows + begin, 128))
            summed[s, pl.ds(begin, 128), :] = total.astype(jnp.bfloat16)
            return 0

        lax.fori_loop(0, rows // 128, step, 0)
        start(("oz", s))

    def finish(s):
        size = 4 * depth
        place = half + s - 2 * half * s

        def step(i, _):
            at = pl.ds(pl.multiple_of(i * 128, 128), 128)
            cols = pl.ds(pl.multiple_of(place * size, 128), size)
            total = own_sum(s, at) + passed[1 - s, at, :].astype(jnp.float32)
            total = panels[side, at, cols].astype(jnp.float32) + total
            block_ref[at, cols] = total.astype(jnp.bfloat16)
            return 0

        lax.fori_loop(0, rows // 128, step, 0)

    def attend(first, count):
        def step(i):
            image, head = lax.div(i, heads), lax.rem(i, heads)
            at = pl.ds(pl.multiple_of(image * PATCHES, PATCHES), PATCHES)

            def pick(group):
                begin = pl.multiple_of(group * head_cols + head * HD, HD)
                return projected[at, pl.ds(begin, HD)]

            one = pl.ds(half * heads + head, 1)
            queries = layer_norm(pick(0), qgain_ref[one, :]).astype(jnp.bfloat16)
            keys = layer_norm(pick(1), kgain_ref[one, :]).astype(jnp.bfloat16)
            values = pick(2).astype(jnp.bfloat16)
            scores = lax.dot_general(
                queries, keys, (((1,), (1,)), ((), ())), preferred_element_type=jnp.float32
            ) * HD ** (-0.5)
            weights = jnp.exp(scores - jnp.max(scores, axis=-1, keepdims=True))
            probs = weights / jnp.sum(weights, axis=-1, keepdims=True)
            mixed = jnp.dot(
                probs.astype(jnp.bfloat16), values, preferred_element_type=jnp.float32
            )
            joined[at, pl.ds(pl.multiple_of(head * HD, HD), HD)] = mixed.astype(jnp.bfloat16)

        def group(i, _):
            for j in range(heads // 2):
                step(first + i * (heads // 2) + j)
            return 0

        lax.fori_loop(0, count // (heads // 2), group, 0)

    def normalise():
        def run(at):
            left = panels[0, at, :].astype(jnp.float32)
            right = panels[1, at, :].astype(jnp.float32)
            total = jnp.sum(left, axis=-1, keepdims=True) + jnp.sum(right, axis=-1, keepdims=True)
            cols = panels.shape[2]
            mean = total / (2 * cols)
            left, right = left - mean, right - mean
            square = jnp.sum(left * left, axis=-1, keepdims=True)
            square = square + jnp.sum(right * right, axis=-1, keepdims=True)
            scale = lax.rsqrt(square / (2 * cols) + 1e-06)
            normed[at, :cols] = (left * scale * gain_ref[:, :cols]).astype(jnp.bfloat16)
            normed[at, cols:] = (right * scale * gain_ref[:, cols:]).astype(jnp.bfloat16)

        by_rows(run, 64)

    own = [pltpu.make_async_copy(tokens_ref, panels.at[side, near], local_sem.at[0])]
    for t in (1, 2):
        own.append(pltpu.make_async_copy(part(t, half), slot(t, z, y, c), local_sem.at[t]))
    first = [
        pltpu.make_async_copy(src, dst, local_sem.at[3 + g])
        for g, src, dst in thirds(half, slot(0, z, y, c))
    ]

    qkv_steps, up_steps = 3 * head_cols // width, hidden // width
    quarter = heads * (tall // PATCHES) // 4

    for k in (1, 2, 3):
        start_z(0, k)
    start("tz", ("tx", 0))
    for copy in first + own:
        copy.start()
    for copy in first:
        copy.wait()
    for t in range(3):
        start(("y", t, 0, 0), ("c", t, 0, 0, 0))
    arrived("tz")
    start(("tx", 1))
    forward_y(0, 0)
    forward_z(0, 1)
    forward_z(0, 2)
    start_z(1, 1)
    start_z(1, 2)
    forward_z(0, 3)
    for copy in own:
        copy.wait()
    arrived(("tx", 0), ("tx", 1))
    normalise()
    forward_y(1, 0)
    forward_y(2, 0)
    forward_z(1, 1)
    forward_z(1, 2)
    start_z(1, 3)
    start_z(2, 1)
    for k in (1, 2, 3):
        forward_y(0, k)
    for k in range(4):
        landed(0, k)
    project(0, qkv_steps)
    attend(0, quarter)
    forward_z(1, 3)
    start_z(2, 2)
    forward_z(2, 1)
    forward_y(1, 1)
    forward_y(1, 2)
    attend(quarter, 3 * quarter)
    forward_y(1, 3)
    for k in range(4):
        landed(1, k)
    third = up_steps // 3
    expand(0, third)
    start(("z", 2, 3, 0))
    forward_y(2, 1)
    expand(third, third)
    forward_z(2, 2)
    start(("z", 2, 3, 1))
    expand(2 * third, up_steps - 2 * third)
    forward_z(2, 3, 0)
    for p in range(2, LAST_PIECES):
        start(("z", 2, 3, p))
    for k in (0, 1):
        landed(2, k)
        reduce(k)
    forward_y(2, 2)
    landed(2, 2)
    reduce(2)
    start(("ox", 0, 1), ("ox", 0, 0))
    for p in range(1, LAST_PIECES):
        forward_z(2, 3, p)
    pass_on(0)
    for p in range(LAST_PIECES):
        forward_y(2, 3, p)
    landed(2, 3)
    reduce(3, (1,))
    start(("ox", 1, 1))
    reduce(3, (0,))
    start(("ox", 1, 0))
    arrived(("ox", 0, 0), ("oz", 0))
    pass_on(1)
    arrived(("ox", 1, 0))
    finish(1)
    arrived(("oz", 1))
    finish(0)
    for copy in copies.values():
        copy.wait_send()


def fused(tokens, ln_gain, w_qkv, w_up, q_gain, k_gain, w_proj, w_down):
    rows, cols = tokens.shape
    depth = w_up.shape[0]
    heads = q_gain.shape[0] // 2
    head_cols, hidden = heads * HD, w_up.shape[1] // 2
    tall, whole, joint = 2 * rows, 16 * depth, head_cols + hidden
    outs = jnp.concatenate(
        [w_proj.reshape(2, head_cols, depth), w_down.reshape(2, hidden, depth)], axis=1
    ).transpose(0, 2, 1)
    bf16, f32 = jnp.bfloat16, jnp.float32
    anywhere, vmem = pl.BlockSpec(memory_space=pl.ANY), pl.BlockSpec(memory_space=pltpu.VMEM)
    return pl.pallas_call(
        fused_kernel,
        out_shape=[
            jax.ShapeDtypeStruct((rows, cols), bf16),
            jax.ShapeDtypeStruct((whole, 3 * head_cols), bf16),
            jax.ShapeDtypeStruct((whole, hidden), bf16),
            jax.ShapeDtypeStruct((whole, joint), bf16),
        ],
        in_specs=[anywhere, vmem, vmem, vmem] + [anywhere] * 5,
        out_specs=[vmem, anywhere, anywhere, anywhere],
        scratch_shapes=[
            pltpu.VMEM((2, tall, cols), bf16),
            pltpu.VMEM((tall, 2 * cols), bf16),
            pltpu.VMEM((tall, 3 * head_cols), f32),
            pltpu.VMEM((tall, joint), bf16),
            pltpu.VMEM((2, whole, 256), bf16),
            pltpu.VMEM((2, 256, joint), bf16),
            pltpu.VMEM((4, tall, 4 * depth), bf16),
            pltpu.VMEM((2, tall, 4 * depth), bf16),
            pltpu.VMEM((2, rows, 4 * depth), bf16),
            pltpu.VMEM((2, rows, 4 * depth), bf16),
            pltpu.SemaphoreType.DMA((SEMAPHORES,)),
            pltpu.SemaphoreType.DMA((SEMAPHORES,)),
            pltpu.SemaphoreType.DMA((6,)),
            pltpu.SemaphoreType.DMA((2,)),
        ],
        compiler_params=pltpu.CompilerParams(
            collective_id=0, has_side_effects=True, vmem_limit_bytes=58 * 2**20
        ),
    )(
        tokens, ln_gain[None], q_gain, k_gain,
        w_qkv[:, 0], w_qkv[:, 1], w_qkv[:, 2], w_up, outs,
    )[0]


def solution(mesh):
    n, sides = mesh.shape["fsdp"], mesh.shape["mp"]
    return jax.shard_map(
        fused if (n, sides) == (16, 2) else gathered,
        mesh=mesh,
        in_specs=(
            P("fsdp", "mp"),
            P(),
            P("fsdp", None, "mp"),
            P("fsdp", "mp"),
            P("mp", None),
            P("mp", None),
            P("mp", "fsdp"),
            P("mp", "fsdp"),
        ),
        out_specs=P("fsdp", "mp"),
        check_vma=False,
    )
```

```python
import jax
import jax.numpy as jnp
from jax import lax
from jax.experimental import pallas as pl
from jax.experimental.pallas import tpu as pltpu
from jax.sharding import PartitionSpec as P

HD = 128
PATCHES = 256
LAST_PIECES = 3
SEMAPHORES = 80


def layer_norm(values, gain):
    mean = jnp.mean(values, axis=-1, keepdims=True)
    centred = values - mean
    variance = jnp.mean(centred * centred, axis=-1, keepdims=True)
    return centred * lax.rsqrt(variance + 1e-06) * gain


def attention(projected, q_gain, k_gain):
    tok_count = projected[0].shape[0]
    heads = q_gain.shape[0]
    images = tok_count // PATCHES
    queries = layer_norm(projected[0].reshape(tok_count, heads, HD), q_gain)
    keys = layer_norm(projected[1].reshape(tok_count, heads, HD), k_gain)
    split = (images, PATCHES, heads, HD)
    queries = queries.astype(jnp.bfloat16).reshape(split)
    keys = keys.astype(jnp.bfloat16).reshape(split)
    values = projected[2].astype(jnp.bfloat16).reshape(split)
    scores = jnp.einsum(
        "iqhd,ikhd->ihqk", queries, keys, preferred_element_type=jnp.float32
    ) * HD ** (-0.5)
    scores = scores - jnp.max(scores, axis=-1, keepdims=True)
    weights = jnp.exp(scores)
    probs = (weights / jnp.sum(weights, axis=-1, keepdims=True)).astype(jnp.bfloat16)
    attended = jnp.einsum("ihqk,ikhd->iqhd", probs, values, preferred_element_type=jnp.float32)
    return attended.astype(jnp.bfloat16).reshape(tok_count, heads * HD)


def gathered(tokens, ln_gain, w_qkv, w_up, q_gain, k_gain, w_proj, w_down):
    rows = tokens.astype(jnp.float32)
    panels = lax.all_gather(tokens, "mp", axis=1, tiled=True)
    normed = layer_norm(panels.astype(jnp.float32), ln_gain).astype(jnp.bfloat16)
    projected = jnp.einsum(
        "td,dca->cta",
        normed,
        lax.all_gather(w_qkv, "fsdp", axis=0, tiled=True),
        preferred_element_type=jnp.float32,
    )
    hidden_pre = jnp.dot(
        normed,
        lax.all_gather(w_up, "fsdp", axis=0, tiled=True),
        preferred_element_type=jnp.float32,
    )
    attended = attention(projected, q_gain, k_gain)
    activated = jax.nn.gelu(hidden_pre, approximate=False).astype(jnp.bfloat16)
    joined = jnp.concatenate([attended, activated], axis=1)
    out_rows = jnp.concatenate([w_proj, w_down], axis=0)
    terms = jnp.dot(
        joined,
        lax.all_gather(out_rows, "fsdp", axis=1, tiled=True),
        preferred_element_type=jnp.float32,
    )
    branches = lax.psum_scatter(
        terms.astype(jnp.bfloat16), "mp", scatter_dimension=1, tiled=True
    ).astype(jnp.float32)
    return (rows + branches).astype(jnp.bfloat16)


def flip(z, k):
    if k == 1:
        return z + 1 - 2 * lax.rem(z, 2)
    if k == 2:
        return z + 2 - 4 * lax.div(z, 2)
    return 3 - z if k == 3 else z


def fused_kernel(
    tokens_ref, gain_ref, qgain_ref, kgain_ref, q_ref, k_ref, v_ref, up_ref, outs_ref,
    block_ref, all_qkv, all_up, all_out,
    panels, normed, projected, joined, in_tile, out_tile, terms_ref, crossed, passed, summed,
    send_sem, recv_sem, local_sem, tile_sem,
):
    me, side = lax.axis_index("fsdp"), lax.axis_index("mp")
    z, y, c = lax.div(me, 4), lax.rem(lax.div(me, 2), 2), lax.rem(me, 2)
    half = lax.rem(z, 2)
    rows = tokens_ref.shape[0]
    depth = up_ref.shape[0]
    heads = qgain_ref.shape[0] // 2
    head_cols = heads * HD
    hidden = up_ref.shape[1] // 2
    tall = 2 * rows
    width = in_tile.shape[2]

    def device(z, y, c):
        return (z * 4 + y * 2 + c, side)

    def remote(index, src, dst, target):
        return pltpu.make_async_remote_copy(
            src_ref=src,
            dst_ref=dst,
            send_sem=send_sem.at[index],
            recv_sem=recv_sem.at[index],
            device_id=target,
            device_id_type=pl.DeviceIdType.MESH,
        )

    def slot(t, z, y, c, piece=0, pieces=1):
        size = depth // pieces
        begin = (z * 4 + y * 2 + c) * depth + piece * size
        return wholes[t].at[pl.ds(pl.multiple_of(begin, size), size)]

    wholes = (all_qkv, all_up, all_out)
    partners = [device(flip(z, k), y, c) for k in (1, 2, 3)]
    partners += [device(z, 1 - y, c), device(z, y, 1 - c), (me, 1 - side)]
    barrier = pltpu.get_barrier_semaphore()
    for partner in partners:
        pl.semaphore_signal(
            barrier, inc=1, device_id=partner, device_id_type=pl.DeviceIdType.MESH
        )
    pl.semaphore_wait(barrier, len(partners))

    def pieces_of(t, k):
        return LAST_PIECES if (t, k) == (2, 3) else 1

    def part(t, which, piece=0, pieces=1):
        if t == 1:
            return up_ref.at[:, pl.ds(pl.multiple_of(which * hidden, 128), hidden)]
        size = depth // pieces
        return outs_ref.at[which, pl.ds(piece * size, size)]

    def thirds(which, into):
        cols = pl.ds(pl.multiple_of(which * head_cols, 128), head_cols)
        for g, ref in enumerate((q_ref, k_ref, v_ref)):
            yield g, ref.at[:, cols], into.at[:, pl.ds(g * head_cols, head_cols)]

    copies = {}

    def add(key, src, dst, target):
        copies[key] = remote(len(copies), src, dst, target)

    for t in range(3):
        for k in range(4):
            target = device(flip(z, k), y, c)
            which = 1 - half if k % 2 else half
            count = pieces_of(t, k)
            if k and t == 0:
                for g, src, dst in thirds(which, slot(0, z, y, c)):
                    add(("z", t, k, g), src, dst, target)
            for p in range(count):
                if k and t:
                    add(("z", t, k, p), part(t, which, p, count), slot(t, z, y, c, p, count), target)
                here = slot(t, flip(z, k), y, c, p, count)
                source = part(t, half) if k == 0 and t else here
                add(("y", t, k, p), source, here, device(z, 1 - y, c))
                add(("c", t, k, p, 0), source, here, device(z, y, 1 - c))
                across = slot(t, flip(z, k), 1 - y, c, p, count)
                add(("c", t, k, p, 1), across, across, device(z, y, 1 - c))
    near, far = pl.ds(0, rows), pl.ds(rows, rows)
    beside, below = (me, 1 - side), device(flip(z, 1), y, c)
    add("tz", tokens_ref, panels.at[side, far], below)
    add(("tx", 0), tokens_ref, panels.at[side, near], beside)
    add(("tx", 1), panels.at[side, far], panels.at[side, far], beside)
    high = lax.div(z, 2)
    keep_low = 1 - high - side + 2 * high * side
    for s in range(2):
        for r, at in ((0, near), (1, far)):
            add(("ox", s, r), terms_ref.at[s + 2 * keep_low, at], crossed.at[s, at], beside)
        add(("oz", s), summed.at[s], passed.at[s], below)
    assert len(copies) <= SEMAPHORES

    def start(*keys):
        for key in keys:
            copies[key].start()

    def arrived(*keys):
        for key in keys:
            copies[key].wait_recv()

    def start_z(t, k):
        start(*[key for key in copies if key[:3] == ("z", t, k)])

    def forward_z(t, k, p=0):
        arrived(*[("z", t, k, g) for g in range(3)] if t == 0 else [("z", t, k, p)])
        start(("y", t, k, p), ("c", t, k, p, 0))

    def forward_y(t, k, p=0):
        arrived(("y", t, k, p))
        start(("c", t, k, p, 1))

    def landed(t, k):
        for p in range(pieces_of(t, k)):
            arrived(("c", t, k, p, 0), ("c", t, k, p, 1))

    def stream(first, count, tiles, source, body):
        def fetch(step):
            which = lax.rem(step, 2)
            return pltpu.make_async_copy(source(step), tiles.at[which], tile_sem.at[which])

        fetch(first).start()

        def step(i, _):
            @pl.when(i + 1 < first + count)
            def _():
                fetch(i + 1).start()

            fetch(i).wait()
            body(i, tiles[lax.rem(i, 2)])
            return 0

        lax.fori_loop(first, first + count, step, 0)

    def by_rows(run, size):
        def step(i, _):
            run(pl.ds(pl.multiple_of(i * size, size), size))
            return 0

        lax.fori_loop(0, tall // size, step, 0)

    def columns(step):
        return pl.ds(pl.multiple_of(step * width, width), width)

    def project(first, count):
        def body(step, tile):
            def run(at):
                projected[at, columns(step)] = jnp.dot(
                    normed[at, :], tile, preferred_element_type=jnp.float32
                )

            by_rows(run, 512)

        stream(first, count, in_tile, lambda i: all_qkv.at[:, columns(i)], body)

    def expand(first, count):
        def body(step, tile):
            def run(at):
                pre = jnp.dot(normed[at, :], tile, preferred_element_type=jnp.float32)
                active = 0.5 * pre * (1.0 + lax.erf(pre * 0.5**0.5))
                into = pl.ds(pl.multiple_of(head_cols + step * width, width), width)
                joined[at, into] = active.astype(jnp.bfloat16)

            run(near)
            run(far)

        stream(first, count, in_tile, lambda i: all_up.at[:, columns(i)], body)

    def reduce(k, halves=(0, 1)):
        tile_rows = out_tile.shape[1]

        def source(i):
            begin = flip(z, k) * (4 * depth) + i * tile_rows
            return all_out.at[pl.ds(pl.multiple_of(begin, tile_rows), tile_rows)]

        def body(step, tile):
            into = pl.ds(pl.multiple_of(step * tile_rows, tile_rows), tile_rows)
            for r in halves:
                at = (near, far)[r]
                terms_ref[k, at, into] = lax.dot_general(
                    joined[at, :], tile, (((1,), (1,)), ((), ())),
                    preferred_element_type=jnp.float32,
                ).astype(jnp.bfloat16)

        stream(0, 4 * depth // tile_rows, out_tile, source, body)

    def own_sum(s, at):
        kept = terms_ref[s + 2 * (1 - keep_low), at, :].astype(jnp.float32)
        return kept + crossed[s, at, :].astype(jnp.float32)

    def pass_on(s):
        arrived(("ox", s, 1))
        start(("ox", s, 0))

        def step(i, _):
            begin = pl.multiple_of(i * 128, 128)
            total = own_sum(s, pl.ds(rows + begin, 128))
            summed[s, pl.ds(begin, 128), :] = total.astype(jnp.bfloat16)
            return 0

        lax.fori_loop(0, rows // 128, step, 0)
        start(("oz", s))

    def finish(s):
        size = 4 * depth
        place = half + s - 2 * half * s

        def step(i, _):
            at = pl.ds(pl.multiple_of(i * 128, 128), 128)
            cols = pl.ds(pl.multiple_of(place * size, 128), size)
            total = own_sum(s, at) + passed[1 - s, at, :].astype(jnp.float32)
            total = panels[side, at, cols].astype(jnp.float32) + total
            block_ref[at, cols] = total.astype(jnp.bfloat16)
            return 0

        lax.fori_loop(0, rows // 128, step, 0)

    def attend(first, count):
        def step(i):
            image, head = lax.div(i, heads), lax.rem(i, heads)
            at = pl.ds(pl.multiple_of(image * PATCHES, PATCHES), PATCHES)

            def pick(group):
                begin = pl.multiple_of(group * head_cols + head * HD, HD)
                return projected[at, pl.ds(begin, HD)]

            one = pl.ds(half * heads + head, 1)
            queries = layer_norm(pick(0), qgain_ref[one, :]).astype(jnp.bfloat16)
            keys = layer_norm(pick(1), kgain_ref[one, :]).astype(jnp.bfloat16)
            values = pick(2).astype(jnp.bfloat16)
            scores = lax.dot_general(
                queries, keys, (((1,), (1,)), ((), ())), preferred_element_type=jnp.float32
            ) * HD ** (-0.5)
            weights = jnp.exp(scores - jnp.max(scores, axis=-1, keepdims=True))
            probs = weights / jnp.sum(weights, axis=-1, keepdims=True)
            mixed = jnp.dot(
                probs.astype(jnp.bfloat16), values, preferred_element_type=jnp.float32
            )
            joined[at, pl.ds(pl.multiple_of(head * HD, HD), HD)] = mixed.astype(jnp.bfloat16)

        def group(i, _):
            for j in range(heads // 2):
                step(first + i * (heads // 2) + j)
            return 0

        lax.fori_loop(0, count // (heads // 2), group, 0)

    def normalise():
        def run(at):
            left = panels[0, at, :].astype(jnp.float32)
            right = panels[1, at, :].astype(jnp.float32)
            total = jnp.sum(left, axis=-1, keepdims=True) + jnp.sum(right, axis=-1, keepdims=True)
            cols = panels.shape[2]
            mean = total / (2 * cols)
            left, right = left - mean, right - mean
            square = jnp.sum(left * left, axis=-1, keepdims=True)
            square = square + jnp.sum(right * right, axis=-1, keepdims=True)
            scale = lax.rsqrt(square / (2 * cols) + 1e-06)
            normed[at, :cols] = (left * scale * gain_ref[:, :cols]).astype(jnp.bfloat16)
            normed[at, cols:] = (right * scale * gain_ref[:, cols:]).astype(jnp.bfloat16)

        by_rows(run, 64)

    own = [pltpu.make_async_copy(tokens_ref, panels.at[side, near], local_sem.at[0])]
    for t in (1, 2):
        own.append(pltpu.make_async_copy(part(t, half), slot(t, z, y, c), local_sem.at[t]))
    first = [
        pltpu.make_async_copy(src, dst, local_sem.at[3 + g])
        for g, src, dst in thirds(half, slot(0, z, y, c))
    ]

    qkv_steps, up_steps = 3 * head_cols // width, hidden // width
    quarter = heads * (tall // PATCHES) // 4

    for k in (1, 2, 3):
        start_z(0, k)
    start("tz", ("tx", 0))
    for copy in first + own:
        copy.start()
    for copy in first:
        copy.wait()
    for t in range(3):
        start(("y", t, 0, 0), ("c", t, 0, 0, 0))
    arrived("tz")
    start(("tx", 1))
    forward_y(0, 0)
    forward_z(0, 1)
    forward_z(0, 2)
    start_z(1, 1)
    start_z(1, 2)
    forward_z(0, 3)
    for copy in own:
        copy.wait()
    arrived(("tx", 0), ("tx", 1))
    normalise()
    forward_y(1, 0)
    forward_y(2, 0)
    forward_z(1, 1)
    forward_z(1, 2)
    start_z(1, 3)
    start_z(2, 1)
    for k in (1, 2, 3):
        forward_y(0, k)
    for k in range(4):
        landed(0, k)
    project(0, qkv_steps)
    attend(0, quarter)
    forward_z(1, 3)
    start_z(2, 2)
    forward_z(2, 1)
    forward_y(1, 1)
    forward_y(1, 2)
    attend(quarter, 3 * quarter)
    forward_y(1, 3)
    for k in range(4):
        landed(1, k)
    third = up_steps // 3
    expand(0, third)
    start(("z", 2, 3, 0))
    forward_y(2, 1)
    expand(third, third)
    forward_z(2, 2)
    start(("z", 2, 3, 1))
    expand(2 * third, up_steps - 2 * third)
    forward_z(2, 3, 0)
    for p in range(2, LAST_PIECES):
        start(("z", 2, 3, p))
    landed(2, 0)
    reduce(0)
    forward_y(2, 2)
    landed(2, 2)
    reduce(2)
    start(("ox", 0, 1))
    landed(2, 1)
    reduce(1)
    last = LAST_PIECES - 1
    for p in range(1, last):
        forward_z(2, 3, p)
        forward_y(2, 3, p - 1)
    forward_z(2, 3, last)
    forward_y(2, 3, last - 1)
    pass_on(0)
    forward_y(2, 3, last)
    landed(2, 3)
    reduce(3, (1,))
    start(("ox", 1, 1))
    reduce(3, (0,))
    arrived(("ox", 0, 0), ("oz", 0))
    pass_on(1)
    arrived(("ox", 1, 0))
    finish(1)
    arrived(("oz", 1))
    finish(0)
    for copy in copies.values():
        copy.wait_send()


def fused(tokens, ln_gain, w_qkv, w_up, q_gain, k_gain, w_proj, w_down):
    rows, cols = tokens.shape
    depth = w_up.shape[0]
    heads = q_gain.shape[0] // 2
    head_cols, hidden = heads * HD, w_up.shape[1] // 2
    tall, whole, joint = 2 * rows, 16 * depth, head_cols + hidden
    outs = jnp.concatenate(
        [w_proj.reshape(2, head_cols, depth), w_down.reshape(2, hidden, depth)], axis=1
    ).transpose(0, 2, 1)
    bf16, f32 = jnp.bfloat16, jnp.float32
    anywhere, vmem = pl.BlockSpec(memory_space=pl.ANY), pl.BlockSpec(memory_space=pltpu.VMEM)
    return pl.pallas_call(
        fused_kernel,
        out_shape=[
            jax.ShapeDtypeStruct((rows, cols), bf16),
            jax.ShapeDtypeStruct((whole, 3 * head_cols), bf16),
            jax.ShapeDtypeStruct((whole, hidden), bf16),
            jax.ShapeDtypeStruct((whole, joint), bf16),
        ],
        in_specs=[anywhere, vmem, vmem, vmem] + [anywhere] * 5,
        out_specs=[vmem, anywhere, anywhere, anywhere],
        scratch_shapes=[
            pltpu.VMEM((2, tall, cols), bf16),
            pltpu.VMEM((tall, 2 * cols), bf16),
            pltpu.VMEM((tall, 3 * head_cols), f32),
            pltpu.VMEM((tall, joint), bf16),
            pltpu.VMEM((2, whole, 256), bf16),
            pltpu.VMEM((2, 256, joint), bf16),
            pltpu.VMEM((4, tall, 4 * depth), bf16),
            pltpu.VMEM((2, tall, 4 * depth), bf16),
            pltpu.VMEM((2, rows, 4 * depth), bf16),
            pltpu.VMEM((2, rows, 4 * depth), bf16),
            pltpu.SemaphoreType.DMA((SEMAPHORES,)),
            pltpu.SemaphoreType.DMA((SEMAPHORES,)),
            pltpu.SemaphoreType.DMA((6,)),
            pltpu.SemaphoreType.DMA((2,)),
        ],
        compiler_params=pltpu.CompilerParams(
            collective_id=0, has_side_effects=True, vmem_limit_bytes=58 * 2**20
        ),
    )(
        tokens, ln_gain[None], q_gain, k_gain,
        w_qkv[:, 0], w_qkv[:, 1], w_qkv[:, 2], w_up, outs,
    )[0]


def solution(mesh):
    n, sides = mesh.shape["fsdp"], mesh.shape["mp"]
    return jax.shard_map(
        fused if (n, sides) == (16, 2) else gathered,
        mesh=mesh,
        in_specs=(
            P("fsdp", "mp"),
            P(),
            P("fsdp", None, "mp"),
            P("fsdp", "mp"),
            P("mp", None),
            P("mp", None),
            P("mp", "fsdp"),
            P("mp", "fsdp"),
        ),
        out_specs=P("fsdp", "mp"),
        check_vma=False,
    )
```
